256 devices in a mesh: row: 32 (over x, z), col: 8 (over y, core).
Axes of the slice: x: 4, y: 4, z: 8, core: 2. Of those that a mesh axis runs over, the one named last changes fastest.
Arguments:
- right_sides: bfloat16 [4, 256, 256, 256], P(None, ('row', 'col')), may hold values from -6 to 6
- lower_blocks: bfloat16 [32, 8, 3, 6, 256, 256], P('row', 'col'), may hold values from -0.1875 to 0.1875
- lower_source: int32 [32, 8, 3, 6], P('row', 'col'), may hold values from 0 to 31
- lower_target: int32 [32, 8, 3, 6], P('row', 'col'), may hold values from 8 to 32, as said below
- diag_lower_inv: bfloat16 [4, 256, 256, 256], P(None, ('row', 'col')), may hold values from -1 to 2, as said below
- upper_blocks: bfloat16 [32, 8, 3, 6, 256, 256], P('row', 'col'), may hold values from -0.1875 to 0.1875
- upper_source: int32 [32, 8, 3, 6], P('row', 'col'), may hold values from 0 to 31
- upper_target: int32 [32, 8, 3, 6], P('row', 'col'), may hold values from 0 to 32, as said below
- diag_upper_inv: bfloat16 [4, 256, 256, 256], P(None, ('row', 'col')), may hold values from -1 to 2, as said below
Outputs:
- solution: float32 [4, 256, 256, 256], P(None, ('row', 'col'))
The draws below stay inside these ranges and needn't reach their ends.
Inputs may be any that keep to these rules, and one draw needn't show every extreme that they name: lower_target[r, c, a, k] is 32 for an empty slot, else b * 8 + q with a < b < 4 and 0 <= q < 8. upper_target[r, c, a, k] is 32 for an empty slot, else b * 8 + q with 0 <= b <= a and 0 <= q < 8. `diag_lower_inv`: each block is lower triangular with a positive diagonal. `diag_upper_inv`: each block is upper triangular with a positive diagonal.
All inputs are finite; a program needn't handle non-finite values.
Results may differ from the reference program's by a relative error of at most 0.029.
Values may be sent and summed in bfloat16 or wider, within the bound.
No kernel may reach another device: no remote copies, remote signals or barrier semaphores. Data moves between devices by JAX's collectives and lax.ppermute only.
A program may use at most 128 MiB of HBM per device.

```python
import math
import jax
import jax.numpy as jnp
from jax import lax

W = 256
RHS = 256
LEV = 4
NB = 6
SPD = 1
PROC_ROWS = 32
PROC_COLS = 8
LOCAL = 8
SOURCES = 32
SUPER = 256


def level_targets(key, is_lower):
    draw_shape = (PROC_ROWS, PROC_COLS, LEV - 1, NB)
    level_key, place_key, live_key = jax.random.split(key, 3)
    source_level = lax.broadcasted_iota(jnp.int32, draw_shape, 2)
    if is_lower:
        target_level = jax.random.randint(level_key, draw_shape, source_level + 1, LEV)
        forced = LOCAL
    else:
        target_level = jax.random.randint(level_key, draw_shape, jnp.zeros(draw_shape, jnp.int32), source_level + 1)
        forced = 0
    position = jax.random.randint(place_key, draw_shape, 0, LOCAL)
    is_live = jax.random.randint(live_key, draw_shape, 0, 5) < 3
    target = jnp.where(is_live, target_level * LOCAL + position, LEV * LOCAL).astype(jnp.int32)
    target = target.at[0, 0, 0, 0].set(forced)
    return target.at[0, 0, 0, NB - 1].set(LEV * LOCAL)


def draw_lower_target(key, part):
    return level_targets(jax.random.fold_in(key, 11), True)


def draw_upper_target(key, part):
    return level_targets(jax.random.fold_in(key, 12), False)


def triangle(key, is_lower):
    draw_shape = (LEV, SUPER, W, W)
    off_key, diag_key = jax.random.split(key)
    row_pos = lax.broadcasted_iota(jnp.int32, draw_shape, 2)
    col_pos = lax.broadcasted_iota(jnp.int32, draw_shape, 3)
    off_diag = jax.random.normal(off_key, draw_shape, jnp.float32) * (0.6 / math.sqrt(W))
    diagonal = jnp.exp(jax.random.uniform(diag_key, draw_shape, jnp.float32, math.log(0.5), math.log(2.0)))
    if is_lower:
        keep_mask = row_pos > col_pos
    else:
        keep_mask = row_pos < col_pos
    values = jnp.where(row_pos == col_pos, diagonal, jnp.where(keep_mask, off_diag, 0.0))
    return values.astype(jnp.bfloat16)


def draw_diag_lower_inv(key, part):
    return triangle(jax.random.fold_in(key, 21), True)


def draw_diag_upper_inv(key, part):
    return triangle(jax.random.fold_in(key, 22), False)


def plant(drawn, rng, low, high):
    shape = drawn.shape
    index_at = [jax.random.randint(jax.random.fold_in(rng, axis), (), 0, shape[axis]) for axis in range(len(shape))]
    drawn = drawn.at[tuple(index_at)].set(low)
    longest = shape.index(max(shape))
    index_at[longest] = (index_at[longest] + 1) % shape[longest]
    return drawn.at[tuple(index_at)].set(high)


def steps_of(rng, shape, shards, low, high):
    gain = 1.0
    for axis_at, blocks in shards:
        steps = jax.random.uniform(jax.random.fold_in(jax.random.fold_in(rng, 6), axis_at), (blocks,), jnp.float32, low / len(shards), high / len(shards))
        gain = gain * jnp.repeat(jnp.exp(steps), shape[axis_at] // blocks).reshape((-1,) + (1,) * (len(shape) - 1 - axis_at))
    return gain


def centred(rng, extent, spread, bound, shards=(), kind=jnp.bfloat16):
    loudness = steps_of(rng, extent, shards, -0.22, 0.18) if shards else 1.0
    drawn = jax.random.normal(rng, extent, jnp.float32) * spread * loudness
    return jnp.minimum(jnp.maximum(drawn, -bound), bound).astype(kind)


def setup_inputs(seed: int = 0) -> dict:
    seeds = jax.random.split(jax.random.key(seed), 10)
    return {
        "right_sides": centred(seeds[0], (LEV, SUPER, W, RHS), 1.0, 6.0, ((1, 256),)),
        "lower_blocks": centred(seeds[1], (PROC_ROWS, PROC_COLS, LEV - 1, NB, W, W), (4 * W) ** -0.5, 0.1875, ((0, 32), (1, 8))),
        "lower_source": plant(jax.random.randint(seeds[2], (PROC_ROWS, PROC_COLS, LEV - 1, NB), 0, SOURCES), jax.random.fold_in(seeds[2], 1), 0, SOURCES - 1).astype(jnp.int32),
        "lower_target": draw_lower_target(jax.random.fold_in(seeds[9], 71), 0),
        "diag_lower_inv": draw_diag_lower_inv(jax.random.fold_in(seeds[9], 71), 0),
        "upper_blocks": centred(seeds[5], (PROC_ROWS, PROC_COLS, LEV - 1, NB, W, W), (4 * W) ** -0.5, 0.1875, ((0, 32), (1, 8))),
        "upper_source": plant(jax.random.randint(seeds[6], (PROC_ROWS, PROC_COLS, LEV - 1, NB), 0, SOURCES), jax.random.fold_in(seeds[6], 1), 0, SOURCES - 1).astype(jnp.int32),
        "upper_target": draw_upper_target(jax.random.fold_in(seeds[9], 71), 0),
        "diag_upper_inv": draw_diag_upper_inv(jax.random.fold_in(seeds[9], 71), 0),
    }


def round_trip(values):
    return lax.optimization_barrier(values.astype(jnp.bfloat16)).astype(jnp.float32)


def row_totals(partial_value, tree_level):
    rounded = round_trip(partial_value[:, :, tree_level])
    row_total = jnp.sum(rounded, axis=1)
    return row_total.reshape(SUPER, W, RHS)


def solve_diag(inverse, vector):
    return jnp.einsum("sij,sjm->sim", inverse.astype(jnp.float32), vector.astype(jnp.float32), precision=lax.Precision.HIGHEST)


def add_level(partial_value, blocks, source, target, solved_panel):
    panel_grid = solved_panel.reshape(PROC_ROWS, PROC_COLS, SPD, W, RHS)
    col_indices = jnp.arange(PROC_COLS, dtype=jnp.int32)

    def one_col(col_blocks, col_source, col_target, col_index):
        chosen = panel_grid[col_source // SPD, col_index, col_source % SPD]
        products = jnp.einsum("kij,kjm->kim", col_blocks.astype(jnp.float32), chosen.astype(jnp.float32), precision=lax.Precision.HIGHEST)
        summed = jax.ops.segment_sum(products, col_target, num_segments=LEV * LOCAL + 1)
        return summed[:LEV * LOCAL]

    def one_row(row_index, accumulated):
        row_blocks = lax.dynamic_index_in_dim(blocks, row_index, 0, keepdims=False)
        row_source = lax.dynamic_index_in_dim(source, row_index, 0, keepdims=False)
        row_target = lax.dynamic_index_in_dim(target, row_index, 0, keepdims=False)
        row_terms = jax.vmap(one_col)(row_blocks, row_source, row_target, col_indices)
        row_terms = row_terms.reshape(PROC_COLS, LEV, LOCAL, W, RHS)
        current = lax.dynamic_index_in_dim(accumulated, row_index, 0, keepdims=False)
        return lax.dynamic_update_index_in_dim(accumulated, current + row_terms, row_index, 0)

    return lax.fori_loop(0, PROC_ROWS, one_row, partial_value)


def reference(right_sides, lower_blocks, lower_source, lower_target, diag_lower_inv, upper_blocks, upper_source, upper_target, diag_upper_inv):
    buffer_shape = (PROC_ROWS, PROC_COLS, LEV, LOCAL, W, RHS)
    partial_value = jnp.zeros(buffer_shape, jnp.float32)
    forward = []
    for tree_level in range(LEV):
        row_total = row_totals(partial_value, tree_level)
        lowered = (right_sides[tree_level].astype(jnp.float32) - row_total).astype(jnp.bfloat16)
        result = solve_diag(diag_lower_inv[tree_level], lowered)
        forward.append(result)
        if tree_level + 1 < LEV:
            partial_value = add_level(partial_value, lower_blocks[:, :, tree_level], lower_source[:, :, tree_level], lower_target[:, :, tree_level], result.astype(jnp.bfloat16))
    partial_value = jnp.zeros(buffer_shape, jnp.float32)
    solution = [None] * LEV
    for tree_level in range(LEV - 1, -1, -1):
        row_total = row_totals(partial_value, tree_level)
        raised = (forward[tree_level] - row_total).astype(jnp.bfloat16)
        result = solve_diag(diag_upper_inv[tree_level], raised)
        solution[tree_level] = result
        if tree_level > 0:
            partial_value = add_level(partial_value, upper_blocks[:, :, tree_level - 1], upper_source[:, :, tree_level - 1], upper_target[:, :, tree_level - 1], result.astype(jnp.bfloat16))
    return jnp.stack(solution)
```

```python
import functools

import jax
import jax.numpy as jnp
from jax import lax
from jax.experimental import pallas as pl
from jax.experimental.pallas import tpu as pltpu
from jax.sharding import PartitionSpec as P

X, Z, Y, C = 4, 8, 4, 2
LOCAL = Y * C
VMEM = pl.BlockSpec(memory_space=pltpu.VMEM)
SMEM = pl.BlockSpec(memory_space=pltpu.SMEM)
ANY = pl.BlockSpec(memory_space=pl.ANY)
PARAMS = pltpu.CompilerParams(vmem_limit_bytes=40 * 1024 * 1024)
NT = (((1,), (1,)), ((), ()))


def dot_nt(a, b):
    return lax.dot_general(a, b, NT, preferred_element_type=jnp.float32)


def along_x(value, d):
    return lax.ppermute(value, "row", [(x * Z + z, (x + d) % X * Z + z) for x in range(X) for z in range(Z)])


def along_z(value, d):
    return lax.ppermute(value, "row", [(x * Z + z, x * Z + (z + d) % Z) for x in range(X) for z in range(Z)])


def along_y(value, d):
    return lax.ppermute(value, "col", [(y * C + k, (y + d) % Y * C + k) for y in range(Y) for k in range(C)])


def other_core(value):
    return lax.ppermute(value, "col", [(y * C + k, y * C + 1 - k) for y in range(Y) for k in range(C)])


def gather_x(value):
    groups = [[x * Z + z for x in range(X)] for z in range(Z)]
    return lax.all_gather(value, "row", axis=0, tiled=True, axis_index_groups=groups)


def ring_pieces(panel):
    up, down = [panel], [panel]
    for _ in range(Z // 2 - 1):
        up.append(along_z(up[-1], 1))
        down.append(along_z(down[-1], -1))
    up.append(along_z(up[-1], 1))
    return up + down[:0:-1]


def update_body(first_level, level_count, slots, per_row, has_start, is_split, *refs):
    place, source, target = refs[:3]
    pieces = refs[3 : 3 + Z]
    blocks = refs[3 + Z]
    rest = refs[4 + Z :]
    if has_start:
        start, rest = rest[0], rest[1:]
    if is_split:
        mine, other, rest = rest[0], rest[1], rest[2:]
    else:
        total, rest = rest[0], rest[1:]
    piece_buf, block_buf, acc, piece_sem, block_sem, acc_sem = rest
    x, z, y, core = place[0], place[1], place[2], place[3]

    def piece_copy(d):
        return pltpu.make_async_copy(pieces[d], piece_buf.at[d], piece_sem.at[d])

    def block_copy(s):
        return pltpu.make_async_copy(
            blocks.at[s // slots * per_row + s % slots], block_buf.at[s], block_sem.at[s]
        )

    def position(s):
        return target[s // slots, s % slots] - first_level * LOCAL

    def is_live(s):
        at = position(s)
        return (at >= 0) & (at < level_count * LOCAL)

    for d in range(Z):
        piece_copy(d).start()
    if has_start:
        start_copy = pltpu.make_async_copy(start, acc, acc_sem)
        start_copy.start()
    for s in range(X * slots):
        pl.when(is_live(s))(lambda s=s: block_copy(s).start())
    if has_start:
        start_copy.wait()
    else:
        acc[...] = jnp.zeros_like(acc)
    for d in range(Z):
        piece_copy(d).wait()
    for s in range(X * slots):

        def add_product(s=s):
            block_copy(s).wait()
            from_row = source[s // slots, s % slots]
            chosen = piece_buf[(z - lax.rem(from_row, Z)) & (Z - 1), (x - lax.div(from_row, Z)) & (X - 1)]
            at, row = position(s), (x - s // slots) & (X - 1)
            acc[at, row] += dot_nt(chosen, block_buf[s])

        pl.when(is_live(s))(add_product)
    if is_split:
        for d in range(Y):
            column = ((y + d) & (Y - 1)) * C
            mine[d] = acc[column + core].astype(mine.dtype)
            other[d] = acc[column + 1 - core].astype(other.dtype)
    else:
        out_copy = pltpu.make_async_copy(acc, total, acc_sem)
        out_copy.start()
        out_copy.wait()


def block_updates(place, source, target, pieces, blocks, first_level, level_count, start, is_split):
    slots = source.shape[1]
    per_row = blocks.shape[0] // X
    panel = pieces[0].shape
    acc_shape = (level_count * LOCAL,) + panel
    if is_split:
        half = jax.ShapeDtypeStruct((Y,) + panel, jnp.bfloat16)
        out_shape, out_specs = (half, half), (VMEM, VMEM)
    else:
        out_shape, out_specs = jax.ShapeDtypeStruct(acc_shape, jnp.float32), ANY
    operands = [place, source, target, *pieces, blocks]
    in_specs = [SMEM] * 3 + [ANY] * (Z + 1)
    if start is not None:
        operands.append(start)
        in_specs.append(ANY)
    body = functools.partial(
        update_body, first_level, level_count, slots, per_row, start is not None, is_split
    )
    return pl.pallas_call(
        body,
        out_shape=out_shape,
        in_specs=in_specs,
        out_specs=out_specs,
        scratch_shapes=[
            pltpu.VMEM((Z,) + panel, jnp.bfloat16),
            pltpu.VMEM((X * slots,) + blocks.shape[1:], jnp.bfloat16),
            pltpu.VMEM(acc_shape, jnp.float32),
            pltpu.SemaphoreType.DMA((Z,)),
            pltpu.SemaphoreType.DMA((X * slots,)),
            pltpu.SemaphoreType.DMA,
        ],
        compiler_params=PARAMS,
        cost_estimate=pl.CostEstimate(flops=400_000_000, bytes_accessed=9_000_000, transcendentals=0),
    )(*operands)


def add_body(mine, theirs, *outs):
    for d in range(Y):
        outs[d][...] = (mine[d].astype(jnp.float32) + theirs[d].astype(jnp.float32)).astype(jnp.bfloat16)


def add_halves(mine, theirs):
    part = jax.ShapeDtypeStruct(mine.shape[1:], mine.dtype)
    return pl.pallas_call(
        add_body,
        out_shape=[part] * Y,
        in_specs=[VMEM] * 2,
        out_specs=[VMEM] * Y,
        compiler_params=PARAMS,
        cost_estimate=pl.CostEstimate(flops=300_000, bytes_accessed=1_500_000, transcendentals=0),
    )(mine, theirs)


def col_total(mine, other):
    sums = add_halves(mine, other_core(other))
    return [sums[0]] + [along_y(sums[d], d) for d in range(1, Y)]


def solve_body(per_row, slots, inverses, keep_result, *refs):
    place = refs[0]
    terms = refs[1 : 1 + Y]
    right, blocks = refs[1 + Y], refs[2 + Y]
    first_out, panel_out, buffer, sem = refs[3 + Y :]
    x = place[0]

    def copy(i, d):
        at = ((x - d) & (X - 1)) * per_row + slots + i
        return pltpu.make_async_copy(blocks.at[at], buffer.at[i * X + d], sem.at[i * X + d])

    for i in range(inverses):
        for d in range(X):
            copy(i, d).start()
    for d in range(X):
        total = sum(term[d].astype(jnp.float32) for term in terms)
        vector = (right[d].astype(jnp.float32) - total).astype(jnp.bfloat16)
        copy(0, d).wait()
        result = dot_nt(vector, buffer[d])
        if inverses == 2:
            vector = result.astype(jnp.bfloat16)
            copy(1, d).wait()
            result = dot_nt(vector, buffer[X + d])
        first_out[d] = result if keep_result else vector
        panel_out[d] = result.astype(jnp.bfloat16)


def diag_solve(place, terms, right, blocks, slots, inverses, keep_result):
    panel = right.shape
    return pl.pallas_call(
        functools.partial(solve_body, blocks.shape[0] // X, slots, inverses, keep_result),
        out_shape=(
            jax.ShapeDtypeStruct(panel, jnp.float32 if keep_result else jnp.bfloat16),
            jax.ShapeDtypeStruct(panel, jnp.bfloat16),
        ),
        in_specs=[SMEM] + [VMEM] * (Y + 1) + [ANY],
        out_specs=(VMEM, VMEM),
        scratch_shapes=[
            pltpu.VMEM((inverses * X,) + blocks.shape[1:], jnp.bfloat16),
            pltpu.SemaphoreType.DMA((inverses * X,)),
        ],
        compiler_params=PARAMS,
        cost_estimate=pl.CostEstimate(flops=33_000_000, bytes_accessed=1_800_000, transcendentals=0),
    )(place, *terms, right, blocks)


def finish_body(levels, has_buffer, has_forward, *refs):
    place = refs[0]
    vectors = refs[1 : 1 + X]
    inverse = refs[1 + X]
    rest = refs[2 + X :]
    if has_forward:
        forward, rest = rest[0], rest[1:]
    if has_buffer:
        rest = rest[1:]
    out, right, result, sem = rest
    rows = vectors[0].shape[1]
    for n, level in enumerate(levels):
        for d in range(X):
            at = pl.ds(pl.multiple_of(((place[0] + d) & (X - 1)) * rows, rows), rows)
            vector = vectors[d][n]
            if has_forward:
                vector = (forward[at, :] - vector.astype(jnp.float32)).astype(jnp.bfloat16)
            right[n, at, :] = vector
        result[n] = dot_nt(inverse[level], right[n])
        pltpu.make_async_copy(result.at[n], out.at[level], sem.at[n]).start()
    for n, level in enumerate(levels):
        pltpu.make_async_copy(result.at[n], out.at[level], sem.at[n]).wait()


def finish(place, vectors, inverse, levels, forward=None, buffer=None):
    width = inverse.shape[1]
    rhs_cols = vectors[0].shape[1] * X
    operands = [place, *vectors, inverse]
    in_specs = [SMEM] + [VMEM] * (X + 1)
    aliases = {}
    if forward is not None:
        operands.append(forward)
        in_specs.append(VMEM)
    if buffer is not None:
        aliases = {len(operands): 0}
        operands.append(buffer)
        in_specs.append(ANY)
    return pl.pallas_call(
        functools.partial(finish_body, levels, buffer is not None, forward is not None),
        out_shape=jax.ShapeDtypeStruct((inverse.shape[0], width, rhs_cols), jnp.float32),
        in_specs=in_specs,
        out_specs=ANY,
        scratch_shapes=[
            pltpu.VMEM((len(levels), rhs_cols, width), jnp.bfloat16),
            pltpu.VMEM((len(levels), width, rhs_cols), jnp.float32),
            pltpu.SemaphoreType.DMA((len(levels),)),
        ],
        input_output_aliases=aliases,
        compiler_params=PARAMS,
        cost_estimate=pl.CostEstimate(
            flops=33_000_000 * len(levels), bytes_accessed=500_000 * len(levels), transcendentals=0
        ),
    )(*operands)


def shards(
    right_sides,
    lower_blocks,
    lower_source,
    lower_target,
    diag_lower_inv,
    upper_blocks,
    upper_source,
    upper_target,
    diag_upper_inv,
):
    levels = right_sides.shape[0]
    slots = lower_blocks.shape[3]
    width, rhs_cols = right_sides.shape[2:]
    top = levels - 1
    row, col = lax.axis_index("row"), lax.axis_index("col")
    x = row // Z
    place = jnp.stack([x, row % Z, col // C, col % C]).astype(jnp.int32)

    where = gather_x(
        jnp.stack([lower_source[0, 0], lower_target[0, 0], upper_source[0, 0], upper_target[0, 0]])[None]
    )
    lower_groups, upper_groups = [], [None] * top
    for level in range(top):
        held = [lower_blocks[0, 0, level], diag_lower_inv[level + 1]]
        if level + 1 == top:
            held.append(diag_upper_inv[top])
        lower_groups.append(gather_x(jnp.concatenate(held)))
    for level in range(top - 1, -1, -1):
        held = [upper_blocks[0, 0, level]]
        if level > 0:
            held.append(diag_upper_inv[level])
        upper_groups[level] = gather_x(jnp.concatenate(held))

    first = jnp.einsum("ij,jm->mi", diag_lower_inv[0, 0], right_sides[0, 0], preferred_element_type=jnp.float32)
    whole = jnp.concatenate([first.astype(jnp.bfloat16)[None], jnp.swapaxes(right_sides[1:, 0], 1, 2)])
    whole = whole.reshape(levels, X, rhs_cols // X, width)
    parts = [lax.dynamic_index_in_dim(whole, (x + d) % X, 1, keepdims=False) for d in range(X)]
    parts = [parts[0]] + [along_x(parts[d], d) for d in range(1, X)]
    rights = [jnp.stack([part[level] for part in parts]) for level in range(levels)]

    panel = rights[0]
    forward = [None] * levels
    later = None
    for level in range(top):
        pieces = ring_pieces(panel)
        source, target, blocks = where[:, 0, level], where[:, 1, level], lower_groups[level]
        start = None if later is None else later[:LOCAL]
        mine, other = block_updates(place, source, target, pieces, blocks, level + 1, 1, start, True)
        if level + 2 < levels:
            rest = None if later is None else later[LOCAL:]
            later = block_updates(
                place, source, target, pieces, blocks, level + 2, levels - level - 2, rest, False
            )
        terms = col_total(mine, other)
        is_top = level + 1 == top
        forward[level + 1], panel = diag_solve(
            place, terms, rights[level + 1], blocks, slots, 2 if is_top else 1, not is_top
        )

    vectors = [None] * levels
    vectors[top] = forward[top]
    later = None
    for level in range(top - 1, -1, -1):
        pieces = ring_pieces(panel)
        source, target, blocks = where[:, 2, level], where[:, 3, level], upper_groups[level]
        start = None if later is None else later[level * LOCAL :]
        mine, other = block_updates(place, source, target, pieces, blocks, level, 1, start, True)
        if level > 0:
            rest = None if later is None else later[: level * LOCAL]
            later = block_updates(place, source, target, pieces, blocks, 0, level, rest, False)
        terms = col_total(mine, other)
        if level > 0:
            vectors[level], panel = diag_solve(place, terms, forward[level], blocks, slots, 1, False)

    upper = [jnp.stack([vectors[level][d] for level in range(1, levels)]) for d in range(X)]
    upper = [upper[0]] + [along_x(upper[d], -d) for d in range(1, X)]
    inverse = diag_upper_inv[:, 0]
    solved = finish(place, upper, inverse, tuple(range(1, levels)))
    total = sum(term.astype(jnp.float32) for term in terms).astype(jnp.bfloat16)
    lowest = [total[d][None] for d in range(X)]
    lowest = [lowest[0]] + [along_x(lowest[d], -d) for d in range(1, X)]
    return finish(place, lowest, inverse, (0,), first, solved)[:, None]


def solution(mesh):
    by_block = P("row", "col", None, None, None, None)
    by_slot = P("row", "col", None, None)
    by_supernode = P(None, ("row", "col"), None, None)
    in_specs = (
        by_supernode,
        by_block,
        by_slot,
        by_slot,
        by_supernode,
        by_block,
        by_slot,
        by_slot,
        by_supernode,
    )
    return jax.shard_map(shards, mesh=mesh, in_specs=in_specs, out_specs=by_supernode, check_vma=False)
```

```python
import functools

import jax
import jax.numpy as jnp
from jax import lax
from jax.experimental import pallas as pl
from jax.experimental.pallas import tpu as pltpu
from jax.sharding import PartitionSpec as P

X, Z, Y, C = 4, 8, 4, 2
LOCAL = Y * C
GROUP = 4
VMEM = pl.BlockSpec(memory_space=pltpu.VMEM)
SMEM = pl.BlockSpec(memory_space=pltpu.SMEM)
ANY = pl.BlockSpec(memory_space=pl.ANY)
PARAMS = pltpu.CompilerParams(vmem_limit_bytes=20 * 1024 * 1024)
NT = (((1,), (1,)), ((), ()))


def dot_nt(a, b):
    return lax.dot_general(a, b, NT, preferred_element_type=jnp.float32)


def along_x(value, d):
    return lax.ppermute(value, "row", [(x * Z + z, (x + d) % X * Z + z) for x in range(X) for z in range(Z)])


def along_z(value, d):
    return lax.ppermute(value, "row", [(x * Z + z, x * Z + (z + d) % Z) for x in range(X) for z in range(Z)])


def along_y(value, d):
    return lax.ppermute(value, "col", [(y * C + k, (y + d) % Y * C + k) for y in range(Y) for k in range(C)])


def other_core(value):
    return lax.ppermute(value, "col", [(y * C + k, y * C + 1 - k) for y in range(Y) for k in range(C)])


def gather_x(value):
    groups = [[x * Z + z for x in range(X)] for z in range(Z)]
    gathered = lax.all_gather(value, "row", axis=0, tiled=True, axis_index_groups=groups)
    return pltpu.with_memory_space_constraint(gathered, pltpu.HBM)


def ring_pieces(panel):
    up, down = [panel], [panel]
    for _ in range(Z // 2 - 1):
        up.append(along_z(up[-1], 1))
        down.append(along_z(down[-1], -1))
    up.append(along_z(up[-1], 1))
    return up + down[:0:-1]


def update_body(level, columns, slots, per_rows, keep, *refs):
    count = len(columns)
    place, table = refs[:2]
    pieces = refs[2 : 2 + Z]
    kept = refs[2 + Z : 1 + Z + count]
    blocks = refs[1 + Z + count : 1 + Z + 2 * count]
    rest = refs[1 + Z + 2 * count :]
    mine, other, rest = rest[0], rest[1], rest[2:]
    if keep:
        held, rest = rest[0], rest[1:]
    block_buf, piece_buf, acc, slot_at, slot_from, block_sem, piece_sem, keep_sem = rest
    x, y, core = place[0], place[2], place[3]
    spare = piece_buf.shape[0] - 1

    def scan(n, found):
        for d in range(X):
            first_block = ((x - d) & (X - 1)) * per_rows[n]

            def visit(k, at, d=d, first_block=first_block):
                entry = table[d, columns[n] + k]
                live = (entry >> 8) == level

                @pl.when(live)
                def _():
                    block = blocks[n].at[first_block + k]
                    pltpu.make_async_copy(block, block_buf.at[at], block_sem.at[at]).start()
                    slot_at[at] = ((entry >> 5) & (LOCAL - 1)) * X + d
                    piece = entry & (X * Z - 1)
                    if n < count - 1:
                        copy = pltpu.make_async_copy(
                            kept[n].at[piece], piece_buf.at[X * Z + at], piece_sem.at[at]
                        )
                        copy.start()
                        slot_from[at] = X * Z + at
                    else:
                        slot_from[at] = piece

                return at + live.astype(jnp.int32)

            for k in range(slots):
                found = visit(k, found)
        return found

    earlier = jnp.int32(0)
    for n in range(count - 1):
        earlier = scan(n, earlier)
    live = scan(count - 1, earlier)
    for d in range(Z):
        piece_buf[d * X : (d + 1) * X] = pieces[d][...]
    if keep:
        keep_copy = pltpu.make_async_copy(piece_buf.at[pl.ds(0, X * Z)], held, keep_sem)
        keep_copy.start()
    acc[...] = jnp.zeros_like(acc)
    piece_buf[spare] = jnp.zeros_like(piece_buf[spare])
    for i in range(GROUP - 1):
        slot_from[live + i] = spare
        slot_at[live + i] = 0

    def add_products(group, carry):
        products = []
        for i in range(GROUP):
            at = group * GROUP + i

            @pl.when(at < live)
            def _():
                pltpu.make_async_copy(blocks[0].at[0], block_buf.at[at], block_sem.at[at]).wait()

            if count > 1:

                @pl.when(at < earlier)
                def _():
                    pltpu.make_async_copy(kept[0].at[0], piece_buf.at[X * Z + at], piece_sem.at[at]).wait()

        for i in range(GROUP):
            at = group * GROUP + i
            block = block_buf[jnp.minimum(at, live - 1)]
            products.append((slot_at[at], dot_nt(piece_buf[slot_from[at]], block)))
        for to, product in products:
            acc[to] += product
        return carry

    lax.fori_loop(0, (live + (GROUP - 1)) // GROUP, add_products, 0)
    for d in range(Y):
        column = ((y + d) & (Y - 1)) * C
        mine[d] = acc[pl.ds((column + core) * X, X)].astype(mine.dtype)
        other[d] = acc[pl.ds((column + 1 - core) * X, X)].astype(other.dtype)
    if keep:
        keep_copy.wait()


def block_updates(place, table, level, columns, slots, pieces, kept, blocks, keep):
    panel = pieces[0].shape
    count = len(columns)
    half = jax.ShapeDtypeStruct((Y,) + panel, jnp.bfloat16)
    held = jax.ShapeDtypeStruct((X * Z,) + panel[1:], jnp.bfloat16)
    total = count * X * slots
    return pl.pallas_call(
        functools.partial(update_body, level, columns, slots, [b.shape[0] // X for b in blocks], keep),
        out_shape=(half, half) + (held,) * keep,
        in_specs=[SMEM] * 2 + [VMEM] * Z + [ANY] * (2 * count - 1),
        out_specs=(VMEM, VMEM) + (ANY,) * keep,
        scratch_shapes=[
            pltpu.VMEM((total,) + blocks[0].shape[1:], jnp.bfloat16),
            pltpu.VMEM((X * Z + total + 1,) + panel[1:], jnp.bfloat16),
            pltpu.VMEM((LOCAL * X,) + panel[1:], jnp.float32),
            pltpu.SMEM((total + GROUP,), jnp.int32),
            pltpu.SMEM((total + GROUP,), jnp.int32),
            pltpu.SemaphoreType.DMA((total,)),
            pltpu.SemaphoreType.DMA((total,)),
            pltpu.SemaphoreType.DMA,
        ],
        compiler_params=PARAMS,
        cost_estimate=pl.CostEstimate(flops=400_000_000, bytes_accessed=9_000_000, transcendentals=0),
    )(place, table, *pieces, *kept, *blocks)


def add_body(mine, theirs, *outs):
    for d in range(Y):
        outs[d][...] = (mine[d].astype(jnp.float32) + theirs[d].astype(jnp.float32)).astype(jnp.bfloat16)


def add_halves(mine, theirs):
    part = jax.ShapeDtypeStruct(mine.shape[1:], mine.dtype)
    return pl.pallas_call(
        add_body,
        out_shape=[part] * Y,
        in_specs=[VMEM] * 2,
        out_specs=[VMEM] * Y,
        compiler_params=PARAMS,
        cost_estimate=pl.CostEstimate(flops=300_000, bytes_accessed=1_500_000, transcendentals=0),
    )(mine, theirs)


def col_total(mine, other):
    sums = add_halves(mine, other_core(other))
    return [sums[0]] + [along_y(sums[d], d) for d in range(1, Y)]


def solve_body(per_row, slots, inverses, start, keep_result, *refs):
    place = refs[0]
    terms = refs[1 : 1 + Y]
    rights = refs[1 + Y : 1 + Y + X]
    blocks, first_out, panel_out, buffer, sem = refs[1 + Y + X :]
    x = place[0]

    def copy(i, d):
        at = ((x - d) & (X - 1)) * per_row + slots + i
        return pltpu.make_async_copy(blocks.at[at], buffer.at[i * X + d], sem.at[i * X + d])

    for i in range(inverses):
        for d in range(X):
            copy(i, d).start()
    for d in range(X):
        total = sum(term[d].astype(jnp.float32) for term in terms)
        right = rights[d][start : start + total.shape[0]].astype(jnp.float32)
        vector = (right - total).astype(jnp.bfloat16)
        copy(0, d).wait()
        result = dot_nt(vector, buffer[d])
        if inverses == 2:
            vector = result.astype(jnp.bfloat16)
            copy(1, d).wait()
            result = dot_nt(vector, buffer[X + d])
        first_out[d] = result if keep_result else vector
        panel_out[d] = result.astype(jnp.bfloat16)


def diag_solve(place, terms, rights, start, blocks, slots, inverses, keep_result):
    panel = terms[0].shape
    return pl.pallas_call(
        functools.partial(solve_body, blocks.shape[0] // X, slots, inverses, start, keep_result),
        out_shape=(
            jax.ShapeDtypeStruct(panel, jnp.float32 if keep_result else jnp.bfloat16),
            jax.ShapeDtypeStruct(panel, jnp.bfloat16),
        ),
        in_specs=[SMEM] + [VMEM] * (Y + X) + [ANY],
        out_specs=(VMEM, VMEM),
        scratch_shapes=[
            pltpu.VMEM((inverses * X,) + blocks.shape[1:], jnp.bfloat16),
            pltpu.SemaphoreType.DMA((inverses * X,)),
        ],
        compiler_params=PARAMS,
        cost_estimate=pl.CostEstimate(flops=33_000_000, bytes_accessed=1_800_000, transcendentals=0),
    )(place, *terms, *rights, blocks)


def begin_body(place, right, inverse, table, first, *rest):
    parts, whole = rest[:X], rest[X]
    levels = right.shape[0]
    rows = whole.shape[1] // X
    result = jnp.dot(inverse[...], right[0], preferred_element_type=jnp.float32).T
    first[...] = result
    whole[0] = result.astype(jnp.bfloat16)
    for level in range(1, levels):
        whole[level] = right[level].astype(jnp.float32).T.astype(jnp.bfloat16)
    for d in range(X):
        at = pl.ds(pl.multiple_of(((place[0] + d) & (X - 1)) * rows, rows), rows)
        for level in range(levels):
            parts[d][level * rows : (level + 1) * rows] = whole[level, at]
        parts[d][levels * rows :] = table[...]


def begin(place, right, inverse, table):
    levels, width, rhs_cols = right.shape
    part = jax.ShapeDtypeStruct((levels * rhs_cols // X + table.shape[0], width), jnp.bfloat16)
    return pl.pallas_call(
        begin_body,
        out_shape=[jax.ShapeDtypeStruct((rhs_cols, width), jnp.float32)] + [part] * X,
        in_specs=[SMEM] + [VMEM] * 3,
        out_specs=[VMEM] * (1 + X),
        scratch_shapes=[pltpu.VMEM((levels, rhs_cols, width), jnp.bfloat16)],
        compiler_params=PARAMS,
        cost_estimate=pl.CostEstimate(flops=33_000_000, bytes_accessed=1_800_000, transcendentals=0),
    )(place, right, inverse, table)


def return_body(*refs):
    terms, vectors, parts = refs[:Y], refs[Y:-X], refs[-X:]
    for d in range(X):
        parts[d][0] = sum(term[d].astype(jnp.float32) for term in terms).astype(jnp.bfloat16)
        for level, vector in enumerate(vectors):
            parts[d][level + 1] = vector[d]


def return_parts(terms, vectors):
    part = jax.ShapeDtypeStruct((1 + len(vectors),) + terms[0].shape[1:], jnp.bfloat16)
    return pl.pallas_call(
        return_body,
        out_shape=[part] * X,
        in_specs=[VMEM] * (Y + len(vectors)),
        out_specs=[VMEM] * X,
        compiler_params=PARAMS,
        cost_estimate=pl.CostEstimate(flops=300_000, bytes_accessed=1_500_000, transcendentals=0),
    )(*terms, *vectors)


def finish_body(place, *refs):
    parts = refs[:X]
    forward, inverse, out, right, result, sem = refs[X:]
    levels, rows = parts[0].shape[:2]
    for level in range(levels):
        for d in range(X):
            at = pl.ds(pl.multiple_of(((place[0] + d) & (X - 1)) * rows, rows), rows)
            vector = parts[d][level]
            if level == 0:
                vector = (forward[at, :] - vector.astype(jnp.float32)).astype(jnp.bfloat16)
            right[level, at, :] = vector
        result[level] = dot_nt(inverse[level], right[level])
        pltpu.make_async_copy(result.at[level], out.at[level], sem.at[level]).start()
    for level in range(levels):
        pltpu.make_async_copy(result.at[level], out.at[level], sem.at[level]).wait()


def finish(place, parts, forward, inverse):
    levels, rows, width = parts[0].shape
    return pl.pallas_call(
        finish_body,
        out_shape=jax.ShapeDtypeStruct((levels, width, rows * X), jnp.float32),
        in_specs=[SMEM] + [VMEM] * (X + 2),
        out_specs=ANY,
        scratch_shapes=[
            pltpu.VMEM((levels, rows * X, width), jnp.bfloat16),
            pltpu.VMEM((levels, width, rows * X), jnp.float32),
            pltpu.SemaphoreType.DMA((levels,)),
        ],
        compiler_params=PARAMS,
        cost_estimate=pl.CostEstimate(flops=130_000_000, bytes_accessed=2_000_000, transcendentals=0),
    )(place, *parts, forward, inverse)


def after(values, token):
    return lax.optimization_barrier((values, token))[0]


def shards(
    right_sides,
    lower_blocks,
    lower_source,
    lower_target,
    diag_lower_inv,
    upper_blocks,
    upper_source,
    upper_target,
    diag_upper_inv,
):
    levels = right_sides.shape[0]
    slots = lower_blocks.shape[3]
    rows, width = right_sides.shape[3] // X, right_sides.shape[2]
    top = levels - 1
    row, col = lax.axis_index("row"), lax.axis_index("col")
    place = jnp.stack([row // Z, row % Z, col // C, col % C]).astype(jnp.int32)

    def lower_group(level, token):
        held = [lower_blocks[0, 0, level], diag_lower_inv[level + 1]]
        if level + 1 == top:
            held.append(diag_upper_inv[top])
        if token is not None:
            held = after(held, token)
        return gather_x(jnp.concatenate(held))

    def upper_group(level, token):
        held = [upper_blocks[0, 0, level]]
        if level > 0:
            held.append(diag_upper_inv[level])
        return gather_x(jnp.concatenate(after(held, token)))

    lower = [lower_group(0, None)]
    upper = [None] * top

    table = jnp.stack([lower_source, lower_target, upper_source, upper_target]).reshape(1, -1)
    entries = table.shape[1]
    table = jnp.pad(table.astype(jnp.bfloat16), ((0, 15), (0, width - entries)))
    first, *parts = begin(place, right_sides[:, 0], diag_lower_inv[0, 0], table)
    parts = [parts[0]] + [along_x(parts[d], d) for d in range(1, X)]
    table = jnp.stack([part[levels * rows, :entries] for part in parts]).astype(jnp.int32)
    table = table.reshape(X, 2, 2, top * slots)
    source, target = table[:, :, 0], table[:, :, 1]
    table = target * (X * Z) + ((place[1] - source) & (Z - 1)) * X + ((place[0] - source // Z) & (X - 1))
    table = table.reshape(X, 2 * top * slots)
    panel = jnp.stack([part[:rows] for part in parts])
    lower.append(lower_group(1, parts[1]))

    def later_groups(step, token):
        if step + 2 < top:
            lower.append(lower_group(step + 2, token))
        elif step + 2 < 2 * top:
            level = 2 * top - step - 3
            upper[level] = upper_group(level, token)

    forward = [None] * levels
    kept = []
    for level in range(top):
        pieces = ring_pieces(panel)
        later_groups(level, pieces[1])
        columns = [n * slots for n in range(level + 1)]
        mine, other, *held = block_updates(
            place, table, level + 1, columns, slots, pieces, kept, lower[: level + 1], level + 1 < top
        )
        kept += held
        terms = col_total(mine, other)
        is_top = level + 1 == top
        forward[level + 1], panel = diag_solve(
            place, terms, parts, (level + 1) * rows, lower[level], slots, 2 if is_top else 1, not is_top
        )

    vectors = [None] * levels
    vectors[top] = forward[top]
    kept = []
    for level in range(top - 1, -1, -1):
        pieces = ring_pieces(panel)
        later_groups(2 * top - 1 - level, pieces[1])
        columns = [(top + n) * slots for n in range(top - 1, level - 1, -1)]
        held_blocks = [upper[n] for n in range(top - 1, level - 1, -1)]
        mine, other, *held = block_updates(
            place, table, level, columns, slots, pieces, kept, held_blocks, level > 0
        )
        kept += held
        terms = col_total(mine, other)
        if level > 0:
            rights = [forward[level][d] for d in range(X)]
            vectors[level], panel = diag_solve(place, terms, rights, 0, upper[level], slots, 1, False)

    back = return_parts(terms, vectors[1:])
    back = [back[0]] + [along_x(back[d], -d) for d in range(1, X)]
    return finish(place, back, first, diag_upper_inv[:, 0])[:, None]


def solution(mesh):
    by_block = P("row", "col", None, None, None, None)
    by_slot = P("row", "col", None, None)
    by_supernode = P(None, ("row", "col"), None, None)
    in_specs = (
        by_supernode,
        by_block,
        by_slot,
        by_slot,
        by_supernode,
        by_block,
        by_slot,
        by_slot,
        by_supernode,
    )
    return jax.shard_map(shards, mesh=mesh, in_specs=in_specs, out_specs=by_supernode, check_vma=False)
```

```python
import functools

import jax
import jax.numpy as jnp
from jax import lax
from jax.experimental import pallas as pl
from jax.experimental.pallas import tpu as pltpu
from jax.sharding import PartitionSpec as P

X, Z, Y, C = 4, 8, 4, 2
LOCAL = Y * C
GROUP = 4
VMEM = pl.BlockSpec(memory_space=pltpu.VMEM)
SMEM = pl.BlockSpec(memory_space=pltpu.SMEM)
ANY = pl.BlockSpec(memory_space=pl.ANY)
NT = (((1,), (1,)), ((), ()))


def params(mebibytes):
    return pltpu.CompilerParams(vmem_limit_bytes=mebibytes * 1024 * 1024)


def dot_nt(a, b):
    return lax.dot_general(a, b, NT, preferred_element_type=jnp.float32)


def along_x(value, d):
    return lax.ppermute(value, "row", [(x * Z + z, (x + d) % X * Z + z) for x in range(X) for z in range(Z)])


def along_z(value, d):
    return lax.ppermute(value, "row", [(x * Z + z, x * Z + (z + d) % Z) for x in range(X) for z in range(Z)])


def along_y(value, d):
    return lax.ppermute(value, "col", [(y * C + k, (y + d) % Y * C + k) for y in range(Y) for k in range(C)])


def other_core(value):
    return lax.ppermute(value, "col", [(y * C + k, y * C + 1 - k) for y in range(Y) for k in range(C)])


def exchange_x(value):
    cut = (value.shape[0] + 1) // 2
    last, following = along_x(value, 1), along_x(value, -1)
    far = along_x(last[:cut], 1), along_x(following[cut:], -1)
    return [hbm(held) for held in (value, last, *far, following)], (last, following)


def block_at(blocks, x, d, k):
    if len(blocks) == 1:
        return blocks[0].at[((x - d) & (X - 1)) * (blocks[0].shape[0] // X) + k]
    value, last, far_low, far_high, following = blocks
    cut = far_low.shape[0]
    if d == 2:
        return far_low.at[k] if k < cut else far_high.at[k - cut]
    return (value, last, None, following)[d].at[k]


def hbm(value):
    return pltpu.with_memory_space_constraint(value, pltpu.HBM)


def gather_x(value):
    groups = [[x * Z + z for x in range(X)] for z in range(Z)]
    gathered = lax.all_gather(value, "row", axis=0, tiled=True, axis_index_groups=groups)
    return [hbm(gathered)]


def after(values, token):
    return lax.optimization_barrier((values, token))[0]


def ring_pieces(panel):
    up, down = [panel], [panel]
    for _ in range(Z // 2 - 1):
        up.append(along_z(up[-1], 1))
        down.append(along_z(down[-1], -1))
    up.append(along_z(up[-1], 1))
    return up + down[:0:-1]


def update_body(level, columns, slots, sizes, keep, *refs):
    count = len(columns)
    place, table = refs[:2]
    pieces = refs[2 : 2 + Z]
    kept = refs[2 + Z : 1 + Z + count]
    rest = refs[1 + Z + count :]
    blocks = []
    for size in sizes:
        blocks.append(rest[:size])
        rest = rest[size:]
    mine, other, rest = rest[0], rest[1], rest[2:]
    if keep:
        held, rest = rest[0], rest[1:]
    block_buf, piece_buf, acc, slot_at, slot_from, block_sem, piece_sem, panel_sem, keep_sem = rest
    x, y, core = place[0], place[2], place[3]
    spare = piece_buf.shape[0] - 1

    def scan(n, found):
        for d in range(X):

            def visit(k, at, d=d):
                entry = table[d, columns[n] + k]
                live = (entry >> 8) == level

                @pl.when(live)
                def _():
                    block = block_at(blocks[n], x, d, k)
                    pltpu.make_async_copy(block, block_buf.at[at], block_sem.at[at]).start()
                    slot_at[at] = ((entry >> 5) & (LOCAL - 1)) * X + d
                    piece = entry & (X * Z - 1)
                    if n < count - 1:
                        copy = pltpu.make_async_copy(
                            kept[n].at[piece], piece_buf.at[X * Z + at], piece_sem.at[at]
                        )
                        copy.start()
                        slot_from[at] = X * Z + at
                    else:
                        slot_from[at] = piece

                return at + live.astype(jnp.int32)

            for k in range(slots):
                found = visit(k, found)
        return found

    def panel_copy(d):
        return pltpu.make_async_copy(pieces[d], piece_buf.at[pl.ds(d * X, X)], panel_sem.at[d])

    for d in range(Z):
        panel_copy(d).start()
    earlier = jnp.int32(0)
    for n in range(count - 1):
        earlier = scan(n, earlier)
    live = scan(count - 1, earlier)
    acc[...] = jnp.zeros_like(acc)
    piece_buf[spare] = jnp.zeros_like(piece_buf[spare])
    for d in range(Z):
        panel_copy(d).wait()
    if keep:
        keep_copy = pltpu.make_async_copy(piece_buf.at[pl.ds(0, X * Z)], held, keep_sem)
        keep_copy.start()
    for i in range(GROUP - 1):
        slot_from[live + i] = spare
        slot_at[live + i] = 0

    def add_products(group, carry):
        products = []
        for i in range(GROUP):
            at = group * GROUP + i

            @pl.when(at < live)
            def _():
                pltpu.make_async_copy(blocks[0][0].at[0], block_buf.at[at], block_sem.at[at]).wait()

            if count > 1:

                @pl.when(at < earlier)
                def _():
                    pltpu.make_async_copy(kept[0].at[0], piece_buf.at[X * Z + at], piece_sem.at[at]).wait()

        for i in range(GROUP):
            at = group * GROUP + i
            block = block_buf[jnp.minimum(at, live - 1)]
            products.append((slot_at[at], dot_nt(piece_buf[slot_from[at]], block)))
        for to, product in products:
            acc[to] += product
        return carry

    lax.fori_loop(0, (live + (GROUP - 1)) // GROUP, add_products, 0)
    for d in range(Y):
        column = ((y + d) & (Y - 1)) * C
        mine[d] = acc[pl.ds((column + core) * X, X)].astype(mine.dtype)
        other[d] = acc[pl.ds((column + 1 - core) * X, X)].astype(other.dtype)
    if keep:
        keep_copy.wait()


def block_updates(place, table, level, columns, slots, pieces, kept, blocks, keep):
    panel = pieces[0].shape
    count = len(columns)
    half = jax.ShapeDtypeStruct((Y,) + panel, jnp.bfloat16)
    held = jax.ShapeDtypeStruct((X * Z,) + panel[1:], jnp.bfloat16)
    total = count * X * slots
    return pl.pallas_call(
        functools.partial(update_body, level, columns, slots, [len(b) for b in blocks], keep),
        out_shape=(half, half) + (held,) * keep,
        in_specs=[SMEM] * 2 + [ANY] * (Z + count - 1 + sum(len(b) for b in blocks)),
        out_specs=(VMEM, VMEM) + (ANY,) * keep,
        scratch_shapes=[
            pltpu.VMEM((total,) + blocks[0][0].shape[1:], jnp.bfloat16),
            pltpu.VMEM((X * Z + total + 1,) + panel[1:], jnp.bfloat16),
            pltpu.VMEM((LOCAL * X,) + panel[1:], jnp.float32),
            pltpu.SMEM((total + GROUP,), jnp.int32),
            pltpu.SMEM((total + GROUP,), jnp.int32),
            pltpu.SemaphoreType.DMA((total,)),
            pltpu.SemaphoreType.DMA((total,)),
            pltpu.SemaphoreType.DMA((Z,)),
            pltpu.SemaphoreType.DMA,
        ],
        compiler_params=params(6 + 5 * count),
        cost_estimate=pl.CostEstimate(flops=400_000_000, bytes_accessed=9_000_000, transcendentals=0),
    )(place, table, *map(hbm, pieces), *map(hbm, kept), *sum(blocks, []))


def pack_body(plan, *refs):
    lower, upper, diag_lower, diag_upper = refs[:4]
    groups, sem = refs[4:-1], refs[-1]
    copies = []
    for group, parts in zip(groups, plan):
        at = 0
        for kind, level in parts:
            source = (lower.at[0, 0, level], upper.at[0, 0, level], diag_lower.at[level], diag_upper.at[level])[kind]
            size = source.shape[0]
            copies.append(pltpu.make_async_copy(source, group.at[pl.ds(at, size)], sem.at[len(copies)]))
            at += size
    for copy in copies:
        copy.start()
    for copy in copies:
        copy.wait()


def pack(plan, lower, upper, diag_lower, diag_upper):
    sizes = [sum(lower.shape[3] if kind < 2 else 1 for kind, _ in parts) for parts in plan]
    groups = pl.pallas_call(
        functools.partial(pack_body, plan),
        out_shape=[jax.ShapeDtypeStruct((size,) + lower.shape[4:], lower.dtype) for size in sizes],
        in_specs=[ANY] * 4,
        out_specs=[ANY] * len(plan),
        scratch_shapes=[pltpu.SemaphoreType.DMA((sum(map(len, plan)),))],
        compiler_params=params(4),
        cost_estimate=pl.CostEstimate(flops=0, bytes_accessed=sum(sizes) * 262_144, transcendentals=0),
    )(hbm(lower), hbm(upper), hbm(diag_lower), hbm(diag_upper))
    return list(groups)


def add_body(mine, theirs, *outs):
    for d in range(Y):
        outs[d][...] = (mine[d].astype(jnp.float32) + theirs[d].astype(jnp.float32)).astype(jnp.bfloat16)


def add_halves(mine, theirs):
    part = jax.ShapeDtypeStruct(mine.shape[1:], mine.dtype)
    return pl.pallas_call(
        add_body,
        out_shape=[part] * Y,
        in_specs=[VMEM] * 2,
        out_specs=[VMEM] * Y,
        compiler_params=params(8),
        cost_estimate=pl.CostEstimate(flops=300_000, bytes_accessed=1_500_000, transcendentals=0),
    )(mine, theirs)


def col_total(mine, other):
    sums = add_halves(mine, other_core(other))
    return [sums[0]] + [along_y(sums[d], d) for d in range(1, Y)]


def solve_body(at, inverses, start, keep_result, *refs):
    place = refs[0]
    terms = refs[1 : 1 + Y]
    rights = refs[1 + Y : 1 + Y + X]
    blocks = refs[1 + Y + X : -4]
    first_out, panel_out, buffer, sem = refs[-4:]
    x = place[0]

    def copy(i, d):
        return pltpu.make_async_copy(block_at(blocks, x, d, at + i), buffer.at[i * X + d], sem.at[i * X + d])

    for i in range(inverses):
        for d in range(X):
            copy(i, d).start()
    for d in range(X):
        total = sum(term[d].astype(jnp.float32) for term in terms)
        right = rights[d][start : start + total.shape[0]].astype(jnp.float32)
        vector = (right - total).astype(jnp.bfloat16)
        copy(0, d).wait()
        result = dot_nt(vector, buffer[d])
        if inverses == 2:
            vector = result.astype(jnp.bfloat16)
            copy(1, d).wait()
            result = dot_nt(vector, buffer[X + d])
        first_out[d] = result if keep_result else vector
        panel_out[d] = result.astype(jnp.bfloat16)


def diag_solve(place, terms, rights, start, blocks, at, inverses, keep_result):
    panel = terms[0].shape
    return pl.pallas_call(
        functools.partial(solve_body, at, inverses, start, keep_result),
        out_shape=(
            jax.ShapeDtypeStruct(panel, jnp.float32 if keep_result else jnp.bfloat16),
            jax.ShapeDtypeStruct(panel, jnp.bfloat16),
        ),
        in_specs=[SMEM] + [VMEM] * (Y + X) + [ANY] * len(blocks),
        out_specs=(VMEM, VMEM),
        scratch_shapes=[
            pltpu.VMEM((inverses * X,) + blocks[0].shape[1:], jnp.bfloat16),
            pltpu.SemaphoreType.DMA((inverses * X,)),
        ],
        compiler_params=params(8),
        cost_estimate=pl.CostEstimate(flops=33_000_000, bytes_accessed=1_800_000, transcendentals=0),
    )(place, *terms, *rights, *blocks)


def begin_body(place, right, inverse, table, first, *rest):
    parts, whole = rest[:X], rest[X]
    levels = right.shape[0]
    rows = whole.shape[1] // X
    result = jnp.dot(inverse[...], right[0], preferred_element_type=jnp.float32).T
    first[...] = result
    whole[0] = result.astype(jnp.bfloat16)
    for level in range(1, levels):
        whole[level] = right[level].astype(jnp.float32).T.astype(jnp.bfloat16)
    for d in range(X):
        at = pl.ds(pl.multiple_of(((place[0] + d) & (X - 1)) * rows, rows), rows)
        for level in range(levels):
            parts[d][level * rows : (level + 1) * rows] = whole[level, at]
        parts[d][levels * rows :] = table[...]


def begin(place, right, inverse, table):
    levels, width, rhs_cols = right.shape
    part = jax.ShapeDtypeStruct((levels * rhs_cols // X + table.shape[0], width), jnp.bfloat16)
    return pl.pallas_call(
        begin_body,
        out_shape=[jax.ShapeDtypeStruct((rhs_cols, width), jnp.float32)] + [part] * X,
        in_specs=[SMEM] + [VMEM] * 3,
        out_specs=[VMEM] * (1 + X),
        scratch_shapes=[pltpu.VMEM((levels, rhs_cols, width), jnp.bfloat16)],
        compiler_params=params(8),
        cost_estimate=pl.CostEstimate(flops=33_000_000, bytes_accessed=1_800_000, transcendentals=0),
    )(place, right, inverse, table)


def return_body(*refs):
    terms, vectors, parts = refs[:Y], refs[Y:-X], refs[-X:]
    for d in range(X):
        parts[d][0] = sum(term[d].astype(jnp.float32) for term in terms).astype(jnp.bfloat16)
        for level, vector in enumerate(vectors):
            parts[d][level + 1] = vector[d]


def return_parts(terms, vectors):
    part = jax.ShapeDtypeStruct((1 + len(vectors),) + terms[0].shape[1:], jnp.bfloat16)
    return pl.pallas_call(
        return_body,
        out_shape=[part] * X,
        in_specs=[VMEM] * (Y + len(vectors)),
        out_specs=[VMEM] * X,
        compiler_params=params(8),
        cost_estimate=pl.CostEstimate(flops=300_000, bytes_accessed=1_500_000, transcendentals=0),
    )(*terms, *vectors)


def finish_body(place, *refs):
    parts = refs[:X]
    forward, inverse, out, right, result, sem = refs[X:]
    levels, rows = parts[0].shape[:2]
    for level in range(levels):
        for d in range(X):
            at = pl.ds(pl.multiple_of(((place[0] + d) & (X - 1)) * rows, rows), rows)
            vector = parts[d][level]
            if level == 0:
                vector = (forward[at, :] - vector.astype(jnp.float32)).astype(jnp.bfloat16)
            right[level, at, :] = vector
        result[level] = dot_nt(inverse[level], right[level])
        pltpu.make_async_copy(result.at[level], out.at[level], sem.at[level]).start()
    for level in range(levels):
        pltpu.make_async_copy(result.at[level], out.at[level], sem.at[level]).wait()


def finish(place, parts, forward, inverse):
    levels, rows, width = parts[0].shape
    return pl.pallas_call(
        finish_body,
        out_shape=jax.ShapeDtypeStruct((levels, width, rows * X), jnp.float32),
        in_specs=[SMEM] + [VMEM] * (X + 2),
        out_specs=ANY,
        scratch_shapes=[
            pltpu.VMEM((levels, rows * X, width), jnp.bfloat16),
            pltpu.VMEM((levels, width, rows * X), jnp.float32),
            pltpu.SemaphoreType.DMA((levels,)),
        ],
        compiler_params=params(8),
        cost_estimate=pl.CostEstimate(flops=130_000_000, bytes_accessed=2_000_000, transcendentals=0),
    )(place, *parts, forward, inverse)


def shards(
    right_sides,
    lower_blocks,
    lower_source,
    lower_target,
    diag_lower_inv,
    upper_blocks,
    upper_source,
    upper_target,
    diag_upper_inv,
):
    levels = right_sides.shape[0]
    slots = lower_blocks.shape[3]
    rows, width = right_sides.shape[3] // X, right_sides.shape[2]
    top = levels - 1
    row, col = lax.axis_index("row"), lax.axis_index("col")
    place = jnp.stack([row // Z, row % Z, col // C, col % C]).astype(jnp.int32)

    factors = (lower_blocks, upper_blocks, diag_lower_inv, diag_upper_inv)
    plan = [[(0, level), (2, level + 1)] for level in range(top)]
    plan[-1].append((3, top))
    plan += [[(1, level), (3, level)] if level else [(1, level)] for level in range(top - 1, -1, -1)]
    first_group, near = exchange_x(pack(plan[:1], *factors)[0])
    held = [
        [factors[kind][0, 0, level] if kind < 2 else factors[kind][level] for kind, level in parts]
        for parts in plan[1:]
    ]
    packed = [jnp.concatenate(parts) for parts in held]
    groups = [first_group]

    table = jnp.stack([lower_source, lower_target, upper_source, upper_target]).reshape(1, -1)
    entries = table.shape[1]
    table = jnp.pad(table.astype(jnp.bfloat16), ((0, 15), (0, width - entries)))
    first, *parts = begin(place, right_sides[:, 0], diag_lower_inv[0, 0], table)
    parts = [parts[0]] + [along_x(parts[d], d) for d in range(1, X)]
    table = jnp.stack([part[levels * rows, :entries] for part in parts]).astype(jnp.int32)
    table = table.reshape(X, 2, 2, top * slots)
    source, target = table[:, :, 0], table[:, :, 1]
    table = target * (X * Z) + ((place[1] - source) & (Z - 1)) * X + ((place[0] - source // Z) & (X - 1))
    table = table.reshape(X, 2 * top * slots)
    panel = after(jnp.stack([part[:rows] for part in parts]), (near, packed))

    def next_group(token):
        if packed:
            groups.append(gather_x(after(packed.pop(0), token)))

    next_group(panel)
    forward = [None] * levels
    kept = []
    for level in range(top):
        pieces = ring_pieces(panel)
        if level > 0:
            next_group(pieces[1])
        columns = [n * slots for n in range(level + 1)]
        mine, other, *held = block_updates(
            place, table, level + 1, columns, slots, pieces, kept, groups[: level + 1], level + 1 < top
        )
        kept += held
        terms = col_total(mine, other)
        is_top = level + 1 == top
        forward[level + 1], panel = diag_solve(
            place, terms, parts, (level + 1) * rows, groups[level], slots, 2 if is_top else 1, not is_top
        )

    vectors = [None] * levels
    vectors[top] = forward[top]
    kept = []
    for level in range(top - 1, -1, -1):
        pieces = ring_pieces(panel)
        next_group(pieces[1])
        columns = [(top + n) * slots for n in range(top - 1, level - 1, -1)]
        held_blocks = groups[top : 2 * top - level]
        mine, other, *held = block_updates(
            place, table, level, columns, slots, pieces, kept, held_blocks, level > 0
        )
        kept += held
        terms = col_total(mine, other)
        if level > 0:
            rights = [forward[level][d] for d in range(X)]
            vectors[level], panel = diag_solve(place, terms, rights, 0, groups[2 * top - 1 - level], slots, 1, False)

    back = return_parts(terms, vectors[1:])
    back = [back[0]] + [along_x(back[d], -d) for d in range(1, X)]
    return finish(place, back, first, diag_upper_inv[:, 0])[:, None]


def solution(mesh):
    by_block = P("row", "col", None, None, None, None)
    by_slot = P("row", "col", None, None)
    by_supernode = P(None, ("row", "col"), None, None)
    in_specs = (
        by_supernode,
        by_block,
        by_slot,
        by_slot,
        by_supernode,
        by_block,
        by_slot,
        by_slot,
        by_supernode,
    )
    return jax.shard_map(shards, mesh=mesh, in_specs=in_specs, out_specs=by_supernode, check_vma=False)
```

```python
import functools

import jax
import jax.numpy as jnp
from jax import lax
from jax.experimental import pallas as pl
from jax.experimental.pallas import tpu as pltpu
from jax.sharding import PartitionSpec as P

X, Z, Y, C = 4, 8, 4, 2
LOCAL = Y * C
GROUP = 4
VMEM = pl.BlockSpec(memory_space=pltpu.VMEM)
SMEM = pl.BlockSpec(memory_space=pltpu.SMEM)
ANY = pl.BlockSpec(memory_space=pl.ANY)
NT = (((1,), (1,)), ((), ()))


def params(mebibytes):
    return pltpu.CompilerParams(vmem_limit_bytes=mebibytes * 1024 * 1024)


def dot_nt(a, b):
    return lax.dot_general(a, b, NT, preferred_element_type=jnp.float32)


def along_x(value, d):
    return lax.ppermute(value, "row", [(x * Z + z, (x + d) % X * Z + z) for x in range(X) for z in range(Z)])


def along_z(value, d):
    return lax.ppermute(value, "row", [(x * Z + z, x * Z + (z + d) % Z) for x in range(X) for z in range(Z)])


def along_y(value, d):
    return lax.ppermute(value, "col", [(y * C + k, (y + d) % Y * C + k) for y in range(Y) for k in range(C)])


def other_core(value):
    return lax.ppermute(value, "col", [(y * C + k, y * C + 1 - k) for y in range(Y) for k in range(C)])


def exchange_x(value):
    cut = (value.shape[0] + 1) // 2
    last, following = along_x(value, 1), along_x(value, -1)
    far = along_x(last[:cut], 1), along_x(following[cut:], -1)
    return [hbm(held) for held in (value, last, *far, following)], (last, following)


def block_at(blocks, x, d, k):
    if len(blocks) == 1:
        return blocks[0].at[((x - d) & (X - 1)) * (blocks[0].shape[0] // X) + k]
    value, last, far_low, far_high, following = blocks
    cut = far_low.shape[0]
    if d == 2:
        return far_low.at[k] if k < cut else far_high.at[k - cut]
    return (value, last, None, following)[d].at[k]


def hbm(value):
    return pltpu.with_memory_space_constraint(value, pltpu.HBM)


def gather_x(value):
    groups = [[x * Z + z for x in range(X)] for z in range(Z)]
    gathered = lax.all_gather(value, "row", axis=0, tiled=True, axis_index_groups=groups)
    return [hbm(gathered)]


def after(values, token):
    return lax.optimization_barrier((values, token))[0]


def ring_pieces(panel):
    up, down = [panel], [panel]
    for _ in range(Z // 2 - 1):
        up.append(along_z(up[-1], 1))
        down.append(along_z(down[-1], -1))
    up.append(along_z(up[-1], 1))
    return up + down[:0:-1]


def update_body(level, columns, slots, sizes, late, *refs):
    count = len(columns)
    place, table = refs[:2]
    rest = refs[2:]
    if late:
        last, rest = rest[0], rest[2:]
    else:
        pieces, rest = rest[: Z - 1], rest[Z - 1 :]
    kept, blocks = [], []
    for _ in range(count - 1):
        kept.append(rest[:Z])
        rest = rest[Z:]
    for size in sizes:
        blocks.append(rest[:size])
        rest = rest[size:]
    if late:
        mine, other, rest = rest[0], rest[1], rest[2:]
    acc, block_buf, piece_buf, slot_at, slot_from, block_sem, piece_sem, panel_sem = rest
    x, y, core = place[0], place[2], place[3]
    spare = piece_buf.shape[0] - 1
    far = Z // 2

    def piece_copy(n, dz, piece, at):
        return pltpu.make_async_copy(
            kept[n][dz].at[piece & (X - 1)], piece_buf.at[X * Z + at], piece_sem.at[at]
        )

    def scan(n, found):
        for d in range(X):
            for k in range(slots):
                entry = table[d, columns[n] + k]
                piece, hop = entry & (X * Z - 1), (entry >> 2) & (Z - 1)
                live = (entry >> 8) == level
                if n == count - 1:
                    live = live & ((hop == far) if late else (hop != far))
                at = found

                @pl.when(live)
                def _(n=n, d=d, k=k, entry=entry, piece=piece, hop=hop, at=at):
                    block = block_at(blocks[n], x, d, k)
                    pltpu.make_async_copy(block, block_buf.at[at], block_sem.at[at]).start()
                    slot_at[at] = ((entry >> 5) & (LOCAL - 1)) * X + d
                    if n < count - 1:
                        slot_from[at] = X * Z + at
                        for dz in range(Z):
                            pl.when(hop == dz)(lambda dz=dz: piece_copy(n, dz, piece, at).start())
                    else:
                        slot_from[at] = piece

                found = found + live.astype(jnp.int32)
        return found

    def panel_copy(n, d):
        return pltpu.make_async_copy(pieces[n], piece_buf.at[pl.ds(d * X, X)], panel_sem.at[n])

    places = [d for d in range(Z) if d != far]
    if not late:
        for n, d in enumerate(places):
            panel_copy(n, d).start()
    earlier = jnp.int32(0)
    for n in range(count - 1):
        earlier = scan(n, earlier)
    live = scan(count - 1, earlier)
    piece_buf[spare] = jnp.zeros_like(piece_buf[spare])
    if late:
        piece_buf[far * X : (far + 1) * X] = last[...]
    else:
        acc[...] = jnp.zeros_like(acc)
        for n, d in enumerate(places):
            panel_copy(n, d).wait()
    for i in range(GROUP - 1):
        slot_from[live + i] = spare
        slot_at[live + i] = 0

    def add_products(group, carry):
        products = []
        for i in range(GROUP):
            at = group * GROUP + i

            @pl.when(at < live)
            def _():
                pltpu.make_async_copy(blocks[0][0].at[0], block_buf.at[at], block_sem.at[at]).wait()

            if count > 1:
                pl.when(at < earlier)(lambda: piece_copy(0, 0, 0, at).wait())

        for i in range(GROUP):
            at = group * GROUP + i
            block = block_buf[jnp.minimum(at, live - 1)]
            products.append((slot_at[at], dot_nt(piece_buf[slot_from[at]], block)))
        for to, product in products:
            acc[to] += product
        return carry

    lax.fori_loop(0, (live + (GROUP - 1)) // GROUP, add_products, 0)
    if late:
        for d in range(Y):
            column = ((y + d) & (Y - 1)) * C
            mine[d] = acc[pl.ds((column + core) * X, X)].astype(mine.dtype)
            other[d] = acc[pl.ds((column + 1 - core) * X, X)].astype(other.dtype)


def update_call(place, table, level, columns, slots, inputs, kept, blocks, late):
    panel = inputs[0].shape
    count = len(columns)
    half = jax.ShapeDtypeStruct((Y,) + panel, jnp.bfloat16)
    totals = jax.ShapeDtypeStruct((LOCAL * X,) + panel[1:], jnp.float32)
    total = count * X * slots
    kept, blocks_in = sum(kept, []), sum(blocks, [])
    return pl.pallas_call(
        functools.partial(update_body, level, columns, slots, [len(b) for b in blocks], late),
        out_shape=(half, half, totals) if late else totals,
        in_specs=[SMEM] * 2
        + [VMEM if late else ANY] * len(inputs)
        + [ANY] * (len(kept) + len(blocks_in)),
        out_specs=(VMEM,) * 3 if late else VMEM,
        input_output_aliases={3: 2} if late else {},
        scratch_shapes=[
            pltpu.VMEM((total,) + blocks[0][0].shape[1:], jnp.bfloat16),
            pltpu.VMEM((X * Z + total + 1,) + panel[1:], jnp.bfloat16),
            pltpu.SMEM((total + GROUP,), jnp.int32),
            pltpu.SMEM((total + GROUP,), jnp.int32),
            pltpu.SemaphoreType.DMA((total,)),
            pltpu.SemaphoreType.DMA((total,)),
            pltpu.SemaphoreType.DMA((Z,)),
        ],
        compiler_params=params(4 + 5 * count),
        cost_estimate=pl.CostEstimate(
            flops=200_000_000, bytes_accessed=3_000_000 if late else 9_000_000, transcendentals=0
        ),
    )(place, table, *inputs, *kept, *blocks_in)


def block_updates(place, table, level, columns, slots, pieces, kept, blocks):
    far = Z // 2
    early = [hbm(piece) for d, piece in enumerate(pieces) if d != far]
    kept = [[hbm(piece) for piece in held] for held in kept]
    acc = update_call(place, table, level, columns, slots, early, kept, blocks, False)
    last = [pieces[far], acc]
    return update_call(place, table, level, columns[-1:], slots, last, [], blocks[-1:], True)[:2]


def pack_body(plan, *refs):
    lower, upper, diag_lower, diag_upper = refs[:4]
    groups, sem = refs[4:-1], refs[-1]
    copies = []
    for group, parts in zip(groups, plan):
        at = 0
        for kind, level in parts:
            source = (lower.at[0, 0, level], upper.at[0, 0, level], diag_lower.at[level], diag_upper.at[level])[kind]
            size = source.shape[0]
            copies.append(pltpu.make_async_copy(source, group.at[pl.ds(at, size)], sem.at[len(copies)]))
            at += size
    for copy in copies:
        copy.start()
    for copy in copies:
        copy.wait()


def pack(plan, lower, upper, diag_lower, diag_upper):
    sizes = [sum(lower.shape[3] if kind < 2 else 1 for kind, _ in parts) for parts in plan]
    groups = pl.pallas_call(
        functools.partial(pack_body, plan),
        out_shape=[jax.ShapeDtypeStruct((size,) + lower.shape[4:], lower.dtype) for size in sizes],
        in_specs=[ANY] * 4,
        out_specs=[ANY] * len(plan),
        scratch_shapes=[pltpu.SemaphoreType.DMA((sum(map(len, plan)),))],
        compiler_params=params(4),
        cost_estimate=pl.CostEstimate(flops=0, bytes_accessed=sum(sizes) * 262_144, transcendentals=0),
    )(hbm(lower), hbm(upper), hbm(diag_lower), hbm(diag_upper))
    return list(groups)


def add_body(mine, theirs, *outs):
    for d in range(Y):
        outs[d][...] = (mine[d].astype(jnp.float32) + theirs[d].astype(jnp.float32)).astype(jnp.bfloat16)


def add_halves(mine, theirs):
    part = jax.ShapeDtypeStruct(mine.shape[1:], mine.dtype)
    return pl.pallas_call(
        add_body,
        out_shape=[part] * Y,
        in_specs=[VMEM] * 2,
        out_specs=[VMEM] * Y,
        compiler_params=params(8),
        cost_estimate=pl.CostEstimate(flops=300_000, bytes_accessed=1_500_000, transcendentals=0),
    )(mine, theirs)


def col_total(mine, other):
    sums = add_halves(mine, other_core(other))
    return [sums[0]] + [along_y(sums[d], d) for d in range(1, Y)]


def solve_body(at, inverses, start, keep_result, *refs):
    place = refs[0]
    terms = refs[1 : 1 + Y]
    rights = refs[1 + Y : 1 + Y + X]
    blocks = refs[1 + Y + X : -4]
    first_out, panel_out, buffer, sem = refs[-4:]
    x = place[0]

    def copy(i, d):
        return pltpu.make_async_copy(block_at(blocks, x, d, at + i), buffer.at[i * X + d], sem.at[i * X + d])

    for i in range(inverses):
        for d in range(X):
            copy(i, d).start()
    for d in range(X):
        total = sum(term[d].astype(jnp.float32) for term in terms)
        right = rights[d][start : start + total.shape[0]].astype(jnp.float32)
        vector = (right - total).astype(jnp.bfloat16)
        copy(0, d).wait()
        result = dot_nt(vector, buffer[d])
        if inverses == 2:
            vector = result.astype(jnp.bfloat16)
            copy(1, d).wait()
            result = dot_nt(vector, buffer[X + d])
        first_out[d] = result if keep_result else vector
        panel_out[d] = result.astype(jnp.bfloat16)


def diag_solve(place, terms, rights, start, blocks, at, inverses, keep_result):
    panel = terms[0].shape
    return pl.pallas_call(
        functools.partial(solve_body, at, inverses, start, keep_result),
        out_shape=(
            jax.ShapeDtypeStruct(panel, jnp.float32 if keep_result else jnp.bfloat16),
            jax.ShapeDtypeStruct(panel, jnp.bfloat16),
        ),
        in_specs=[SMEM] + [VMEM] * (Y + X) + [ANY] * len(blocks),
        out_specs=(VMEM, VMEM),
        scratch_shapes=[
            pltpu.VMEM((inverses * X,) + blocks[0].shape[1:], jnp.bfloat16),
            pltpu.SemaphoreType.DMA((inverses * X,)),
        ],
        compiler_params=params(8),
        cost_estimate=pl.CostEstimate(flops=33_000_000, bytes_accessed=1_800_000, transcendentals=0),
    )(place, *terms, *rights, *blocks)


def begin_body(place, right, inverse, table, first, *rest):
    parts, whole = rest[:X], rest[X]
    levels = right.shape[0]
    rows = whole.shape[1] // X
    result = jnp.dot(inverse[...], right[0], preferred_element_type=jnp.float32).T
    first[...] = result
    whole[0] = result.astype(jnp.bfloat16)
    for level in range(1, levels):
        whole[level] = right[level].astype(jnp.float32).T.astype(jnp.bfloat16)
    for d in range(X):
        at = pl.ds(pl.multiple_of(((place[0] + d) & (X - 1)) * rows, rows), rows)
        for level in range(levels):
            parts[d][level * rows : (level + 1) * rows] = whole[level, at]
        parts[d][levels * rows :] = table[...]


def begin(place, right, inverse, table):
    levels, width, rhs_cols = right.shape
    part = jax.ShapeDtypeStruct((levels * rhs_cols // X + table.shape[0], width), jnp.bfloat16)
    return pl.pallas_call(
        begin_body,
        out_shape=[jax.ShapeDtypeStruct((rhs_cols, width), jnp.float32)] + [part] * X,
        in_specs=[SMEM] + [VMEM] * 3,
        out_specs=[VMEM] * (1 + X),
        scratch_shapes=[pltpu.VMEM((levels, rhs_cols, width), jnp.bfloat16)],
        compiler_params=params(8),
        cost_estimate=pl.CostEstimate(flops=33_000_000, bytes_accessed=1_800_000, transcendentals=0),
    )(place, right, inverse, table)


def return_body(*refs):
    terms, vectors, parts = refs[:Y], refs[Y:-X], refs[-X:]
    for d in range(X):
        parts[d][0] = sum(term[d].astype(jnp.float32) for term in terms).astype(jnp.bfloat16)
        for level, vector in enumerate(vectors):
            parts[d][level + 1] = vector[d]


def return_parts(terms, vectors):
    part = jax.ShapeDtypeStruct((1 + len(vectors),) + terms[0].shape[1:], jnp.bfloat16)
    return pl.pallas_call(
        return_body,
        out_shape=[part] * X,
        in_specs=[VMEM] * (Y + len(vectors)),
        out_specs=[VMEM] * X,
        compiler_params=params(8),
        cost_estimate=pl.CostEstimate(flops=300_000, bytes_accessed=1_500_000, transcendentals=0),
    )(*terms, *vectors)


def finish_body(place, *refs):
    parts = refs[:X]
    forward, inverse, out, right, result, sem = refs[X:]
    levels, rows = parts[0].shape[:2]
    for level in range(levels):
        for d in range(X):
            at = pl.ds(pl.multiple_of(((place[0] + d) & (X - 1)) * rows, rows), rows)
            vector = parts[d][level]
            if level == 0:
                vector = (forward[at, :] - vector.astype(jnp.float32)).astype(jnp.bfloat16)
            right[level, at, :] = vector
        result[level] = dot_nt(inverse[level], right[level])
        pltpu.make_async_copy(result.at[level], out.at[level], sem.at[level]).start()
    for level in range(levels):
        pltpu.make_async_copy(result.at[level], out.at[level], sem.at[level]).wait()


def finish(place, parts, forward, inverse):
    levels, rows, width = parts[0].shape
    return pl.pallas_call(
        finish_body,
        out_shape=jax.ShapeDtypeStruct((levels, width, rows * X), jnp.float32),
        in_specs=[SMEM] + [VMEM] * (X + 2),
        out_specs=ANY,
        scratch_shapes=[
            pltpu.VMEM((levels, rows * X, width), jnp.bfloat16),
            pltpu.VMEM((levels, width, rows * X), jnp.float32),
            pltpu.SemaphoreType.DMA((levels,)),
        ],
        compiler_params=params(8),
        cost_estimate=pl.CostEstimate(flops=130_000_000, bytes_accessed=2_000_000, transcendentals=0),
    )(place, *parts, forward, inverse)


def shards(
    right_sides,
    lower_blocks,
    lower_source,
    lower_target,
    diag_lower_inv,
    upper_blocks,
    upper_source,
    upper_target,
    diag_upper_inv,
):
    levels = right_sides.shape[0]
    slots = lower_blocks.shape[3]
    rows, width = right_sides.shape[3] // X, right_sides.shape[2]
    top = levels - 1
    row, col = lax.axis_index("row"), lax.axis_index("col")
    place = jnp.stack([row // Z, row % Z, col // C, col % C]).astype(jnp.int32)

    factors = (lower_blocks, upper_blocks, diag_lower_inv, diag_upper_inv)
    plan = [[(0, level), (2, level + 1)] for level in range(top)]
    plan[-1].append((3, top))
    plan += [[(1, level), (3, level)] if level else [(1, level)] for level in range(top - 1, -1, -1)]
    first_group, near = exchange_x(pack(plan[:1], *factors)[0])
    held = [
        [factors[kind][0, 0, level] if kind < 2 else factors[kind][level] for kind, level in parts]
        for parts in plan[1:]
    ]
    packed = [jnp.concatenate(parts) for parts in held]
    groups = [first_group]

    table = jnp.stack([lower_source, lower_target, upper_source, upper_target]).reshape(1, -1)
    entries = table.shape[1]
    table = jnp.pad(table.astype(jnp.bfloat16), ((0, 15), (0, width - entries)))
    first, *parts = begin(place, right_sides[:, 0], diag_lower_inv[0, 0], table)
    parts = [parts[0]] + [along_x(parts[d], d) for d in range(1, X)]
    table = jnp.stack([part[levels * rows, :entries] for part in parts]).astype(jnp.int32)
    table = table.reshape(X, 2, 2, top * slots)
    source, target = table[:, :, 0], table[:, :, 1]
    table = target * (X * Z) + ((place[1] - source) & (Z - 1)) * X + ((place[0] - source // Z) & (X - 1))
    table = table.reshape(X, 2 * top * slots)
    panel = after(jnp.stack([part[:rows] for part in parts]), (near, packed))

    def next_group(token):
        if packed:
            groups.append(gather_x(after(packed.pop(0), token)))

    next_group(panel)
    forward = [None] * levels
    kept = []
    for level in range(top):
        pieces = ring_pieces(panel)
        if level > 0:
            next_group(pieces[1])
        columns = [n * slots for n in range(level + 1)]
        mine, other = block_updates(
            place, table, level + 1, columns, slots, pieces, kept, groups[: level + 1]
        )
        kept.append(pieces)
        terms = col_total(mine, other)
        is_top = level + 1 == top
        forward[level + 1], panel = diag_solve(
            place, terms, parts, (level + 1) * rows, groups[level], slots, 2 if is_top else 1, not is_top
        )

    vectors = [None] * levels
    vectors[top] = forward[top]
    kept = []
    for level in range(top - 1, -1, -1):
        pieces = ring_pieces(panel)
        next_group(pieces[1])
        columns = [(top + n) * slots for n in range(top - 1, level - 1, -1)]
        held_blocks = groups[top : 2 * top - level]
        mine, other = block_updates(place, table, level, columns, slots, pieces, kept, held_blocks)
        kept.append(pieces)
        terms = col_total(mine, other)
        if level > 0:
            rights = [forward[level][d] for d in range(X)]
            vectors[level], panel = diag_solve(place, terms, rights, 0, groups[2 * top - 1 - level], slots, 1, False)

    back = return_parts(terms, vectors[1:])
    back = [back[0]] + [along_x(back[d], -d) for d in range(1, X)]
    return finish(place, back, first, diag_upper_inv[:, 0])[:, None]


def solution(mesh):
    by_block = P("row", "col", None, None, None, None)
    by_slot = P("row", "col", None, None)
    by_supernode = P(None, ("row", "col"), None, None)
    in_specs = (
        by_supernode,
        by_block,
        by_slot,
        by_slot,
        by_supernode,
        by_block,
        by_slot,
        by_slot,
        by_supernode,
    )
    return jax.shard_map(shards, mesh=mesh, in_specs=in_specs, out_specs=by_supernode, check_vma=False)
```
